32 devices in a mesh: dp: 16 (over z, y, core), fsdp: 2 (over x).
Axes of the slice: x: 2, y: 2, z: 4, core: 2. Of those that a mesh axis runs over, the one named last changes fastest.
Arguments:
- tokens: bfloat16 [24576, 1024], P(('dp', 'fsdp')), may hold values from -6 to 6
- lengths: int32 [64, 3], P(('dp', 'fsdp')), may hold values from 1 to 288, 384 in all within a row
- cotangent: bfloat16 [24576, 1024], P(('dp', 'fsdp')), may hold values from -6 to 6
- qkv_weight: bfloat16 [1024, 3072], P(('dp', 'fsdp')), may hold values from -0.1875 to 0.1875
- query_value_bias: bfloat16 [2048], P(('dp', 'fsdp')), may hold values from -1.5 to 1.5
- dense_weight: bfloat16 [1024, 1024], P(('dp', 'fsdp')), may hold values from -0.5 to 0.5
- dense_bias: bfloat16 [1024], P(('dp', 'fsdp')), may hold values from -1.5 to 1.5
- up_weight: bfloat16 [1024, 4096], P(('dp', 'fsdp')), may hold values from -0.1875 to 0.1875
- up_bias: bfloat16 [4096], P(('dp', 'fsdp')), may hold values from -2.5 to 2.5
- down_weight: bfloat16 [4096, 1024], P(('dp', 'fsdp')), may hold values from -0.09375 to 0.09375
- down_bias: bfloat16 [1024], P(('dp', 'fsdp')), may hold values from -1.5 to 1.5
- norm1_gain: bfloat16 [1024], P(('dp', 'fsdp')), may hold values from 0.099609375 to 1.8984375
- norm1_shift: bfloat16 [1024], P(('dp', 'fsdp')), may hold values from -1.5 to 1.5
- norm2_gain: bfloat16 [1024], P(('dp', 'fsdp')), may hold values from 0.099609375 to 1.8984375
- norm2_shift: bfloat16 [1024], P(('dp', 'fsdp')), may hold values from -1.5 to 1.5
Outputs:
- mixed: bfloat16 [24576, 1024], P(('dp', 'fsdp'))
- input_grad: float32 [24576, 1024], P(('dp', 'fsdp'))
- grad_qkv_weight: float32 [1024, 3072], P(('dp', 'fsdp'))
- grad_query_value_bias: float32 [2048], P(('dp', 'fsdp'))
- grad_dense_weight: float32 [1024, 1024], P(('dp', 'fsdp'))
- grad_dense_bias: float32 [1024], P(('dp', 'fsdp'))
- grad_up_weight: float32 [1024, 4096], P(('dp', 'fsdp'))
- grad_up_bias: float32 [4096], P(('dp', 'fsdp'))
- grad_down_weight: float32 [4096, 1024], P(('dp', 'fsdp'))
- grad_down_bias: float32 [1024], P(('dp', 'fsdp'))
- grad_norm1_gain: float32 [1024], P(('dp', 'fsdp'))
- grad_norm1_shift: float32 [1024], P(('dp', 'fsdp'))
- grad_norm2_gain: float32 [1024], P(('dp', 'fsdp'))
- grad_norm2_shift: float32 [1024], P(('dp', 'fsdp'))
The draws below stay inside these ranges and needn't reach their ends.
Inputs may be any that keep to these rules, and one draw needn't show every extreme that they name: The 3 lengths of each buffer sum to 384; the largest is exactly 288, so the other two together hold 96 tokens.
All inputs are finite; a program needn't handle non-finite values.
Results may differ from the reference program's by a relative error of at most 0.0095.
Values may be sent and summed in bfloat16 or wider, within the bound.
A program may use at most 256 MiB of HBM per device.

```python
import math
import jax
import jax.numpy as jnp
import numpy as np
from jax import lax

D = 1024
HEADS = 16
FF = 4096
MB = 384
SEQS = 3
MOST = 288
BUFFERS = 64
TOKENS = 24576


def raised(array, key, source, target, shards_of, factor):
    owner, partner = [(jnp.arange(array.shape[dim]) // (array.shape[dim] // shards_of)).reshape([-1 if axis == dim else 1 for axis in range(array.ndim)]) for dim in (source, target)]
    chosen = jax.random.permutation(key, shards_of)[partner]
    strong = (owner == chosen) | (owner == (partner + shards_of // 2) % shards_of)
    return jnp.where(strong, factor * array, array)


def shard_levels(key, dims, split, least, high):
    level = 1.0
    for axis_at, blocks in split:
        draws = jax.random.uniform(jax.random.fold_in(jax.random.fold_in(key, 6), axis_at), (blocks,), jnp.float32, least / len(split), high / len(split))
        level = level * jnp.repeat(jnp.exp(draws), dims[axis_at] // blocks).reshape((-1,) + (1,) * (len(dims) - 1 - axis_at))
    return level


def length_profile(amount, total, limit, skew):
    weights = [(1 << 20) // math.isqrt(grade ** skew) + 1 for grade in range(2, amount + 1)]
    rest, holding = total - limit - (amount - 1), [1] * (amount - 1)
    while rest > 0:
        candidates = [i for i in range(amount - 1) if holding[i] < limit]
        pool, left = sum([weights[i] for i in candidates]), rest
        for i in candidates:
            addition = min(limit - holding[i], max(1, left * weights[i] // pool), rest)
            holding[i] = holding[i] + addition
            rest = rest - addition
    return np.array([limit] + holding)


def ragged_sizes(stream_key, count, total, limit, lean):
    if count == 2:
        one = jax.random.randint(stream_key, (), max(1, total - limit), min(limit, total - 1) + 1)
        return jnp.stack([one, total - one])
    sizes = jnp.asarray(length_profile(count, total, limit, lean), jnp.int32)
    couples = (count - 1) // 2
    donor, sink = sizes[1:1 + 2 * couples:2], sizes[2:2 + 2 * couples:2]
    margin = jnp.minimum(donor - 1, limit - sink)
    moved = jax.random.randint(jax.random.fold_in(stream_key, 1), (couples,), 0, 1 << 20) % (margin + 1)
    sizes = sizes.at[1:1 + 2 * couples:2].set(donor - moved).at[2:2 + 2 * couples:2].set(sink + moved)
    return sizes[jax.random.permutation(jax.random.fold_in(stream_key, 2), count)]


def scatter_about(stream_key, shape, scale, most, cuts=(), held_as=jnp.bfloat16):
    drawn = scale * jax.random.normal(stream_key, shape, jnp.float32)
    if cuts:
        drawn = drawn * shard_levels(stream_key, shape, cuts, -0.22, 0.18)
    return jnp.clip(drawn, -most, most).astype(held_as)


def noise_with(stream_key, shape, spread, bound, split, heavy, held_as=jnp.bfloat16):
    values = spread * jax.random.normal(stream_key, shape, jnp.float32)
    if split:
        values = values * shard_levels(stream_key, shape, split, -0.22, 0.18)
    return jnp.clip(raised(values, jax.random.fold_in(stream_key, 3), *heavy), -bound, bound).astype(held_as)


def setup_inputs(seed: int = 0) -> dict:
    arg_keys = jax.random.split(jax.random.key(seed), 16)
    return {
        "tokens": scatter_about(arg_keys[0], (TOKENS, D), 1.0, 6.0, ((0, 32),)),
        "lengths": jax.vmap(lambda own: ragged_sizes(own, SEQS, MB, MOST, 2))(jax.random.split(arg_keys[1], BUFFERS)).reshape((BUFFERS, SEQS)).astype(jnp.int32),
        "cotangent": noise_with(arg_keys[2], (TOKENS, D), 1.0, 6.0, ((0, 32),), (0, 1, 32, 2.75)),
        "qkv_weight": scatter_about(arg_keys[3], (D, 3 * D), D ** -0.5, 0.1875, ((0, 32),)),
        "query_value_bias": scatter_about(arg_keys[4], (2 * D,), 0.3, 1.5, ((0, 32),)),
        "dense_weight": scatter_about(arg_keys[5], (D, D), (D // 8) ** -0.5, 0.5, ((0, 32),)),
        "dense_bias": scatter_about(arg_keys[6], (D,), 0.3, 1.5, ((0, 32),)),
        "up_weight": scatter_about(arg_keys[7], (D, FF), D ** -0.5, 0.1875, ((0, 32),)),
        "up_bias": scatter_about(arg_keys[8], (FF,), 0.5, 2.5, ((0, 32),)),
        "down_weight": scatter_about(arg_keys[9], (FF, D), FF ** -0.5, 0.09375, ((0, 32),)),
        "down_bias": scatter_about(arg_keys[10], (D,), 0.3, 1.5, ((0, 32),)),
        "norm1_gain": jnp.clip(1.0 + 0.18 * jax.random.normal(arg_keys[11], (D,), jnp.float32), 0.099609375, 1.8984375).astype(jnp.bfloat16),
        "norm1_shift": scatter_about(arg_keys[12], (D,), 0.3, 1.5, ((0, 32),)),
        "norm2_gain": jnp.clip(1.0 + 0.18 * jax.random.normal(arg_keys[13], (D,), jnp.float32), 0.099609375, 1.8984375).astype(jnp.bfloat16),
        "norm2_shift": scatter_about(arg_keys[14], (D,), 0.3, 1.5, ((0, 32),)),
    }


@jax.custom_vjp
def low(v):
    return lax.optimization_barrier(v.astype(jnp.bfloat16)).astype(jnp.float32)

@jax.custom_vjp
def low_back(v):
    return v

def low_keep(v):
    return (low(v), None)

def low_pass(kept, grad):
    return (grad,)

def back_keep(v):
    return (v, None)

def back_low(kept, grad):
    return (low(grad),)
low.defvjp(low_keep, low_pass)
low_back.defvjp(back_keep, back_low)
epsilon = 1e-05
masked_score = -1e+30

def matmul(left_side, right_side):
    return jnp.dot(left_side, right_side, precision=lax.Precision.HIGHEST, preferred_element_type=jnp.float32)

def normalize(values, scaling, offset_vec):
    row_mean = lax.optimization_barrier(jnp.mean(values, axis=-1, keepdims=True))
    centred = values - row_mean
    variance = lax.optimization_barrier(jnp.mean(centred * centred, axis=-1, keepdims=True))
    return centred * lax.rsqrt(variance + epsilon) * scaling + offset_vec

def attention_masks(lengths_row, block_rows, heads_count):
    positions = jnp.arange(block_rows, dtype=jnp.int32)
    boundaries = jnp.cumsum(lengths_row.astype(jnp.int32))
    segments = lax.optimization_barrier(jnp.sum((positions[:, None] >= boundaries[None, :]).astype(jnp.int32), axis=1))
    visible = (segments[:, None] == segments[None, :]) & (positions[None, :] <= positions[:, None])
    head_slopes = jnp.exp2(-8.0 * jnp.arange(1, heads_count + 1, dtype=jnp.float32) / heads_count)
    distance = (positions[None, :] - positions[:, None]).astype(jnp.float32)
    alibi_bias = head_slopes[:, None, None] * distance[None, :, :]
    return (visible, alibi_bias)

def layer(inputs, params, visible, alibi_bias):
    w_qkv, b_qv, w_dense, b_dense, w_up, b_up, w_down, b_down, gain_one, shift_one, gain_two, shift_two = params
    block_rows = inputs.shape[0]
    model_width = inputs.shape[1]
    head_dim = model_width // HEADS
    score_scale = 1.0 / math.sqrt(head_dim)
    normed_one = low(normalize(inputs, gain_one, shift_one))
    bias_full = jnp.concatenate([b_qv[:model_width], jnp.zeros((model_width,), jnp.float32), b_qv[model_width:]])
    projected = low(low_back(matmul(normed_one, w_qkv)) + bias_full)
    queries = projected[:, :model_width].reshape(block_rows, HEADS, head_dim)
    keys_all = projected[:, model_width:2 * model_width].reshape(block_rows, HEADS, head_dim)
    values_all = projected[:, 2 * model_width:].reshape(block_rows, HEADS, head_dim)
    products = low_back(jnp.einsum('qhd,khd->hqk', queries, keys_all, precision=lax.Precision.HIGHEST))
    scores = jnp.where(visible[None], products * score_scale + alibi_bias, masked_score)
    row_peak = lax.optimization_barrier(jnp.max(scores, axis=-1, keepdims=True))
    exponent = jnp.exp(scores - row_peak)
    softmaxed = low(exponent / lax.optimization_barrier(jnp.sum(exponent, axis=-1, keepdims=True)))
    attended = jnp.einsum('hqk,khd->qhd', softmaxed, values_all, precision=lax.Precision.HIGHEST)
    attended = low(low_back(attended.reshape(block_rows, model_width)))
    residual_mid = inputs + (low_back(matmul(attended, w_dense)) + b_dense)
    normed_two = low(normalize(residual_mid, gain_two, shift_two))
    upper_pre = low_back(matmul(normed_two, w_up)) + b_up
    activated = low(jax.nn.gelu(upper_pre, approximate=True))
    return residual_mid + (low_back(matmul(activated, w_down)) + b_down)

def reference(tokens, lengths, cotangent, qkv_weight, query_value_bias, dense_weight, dense_bias, up_weight, up_bias, down_weight, down_bias, norm1_gain, norm1_shift, norm2_gain, norm2_shift):
    params = tuple((part.astype(jnp.float32) for part in (qkv_weight, query_value_bias, dense_weight, dense_bias, up_weight, up_bias, down_weight, down_bias, norm1_gain, norm1_shift, norm2_gain, norm2_shift)))
    inputs_all = tokens.astype(jnp.float32).reshape(-1, MB, D)
    cotangents = cotangent.astype(jnp.float32).reshape(-1, MB, D)
    lengths_all = lengths.reshape(-1, SEQS)

    def advance(gradient_sums, bundle):
        inputs, cot_rows, lengths_row = bundle
        visible, alibi_bias = attention_masks(lengths_row, MB, HEADS)

        def forward(values, weights):
            return layer(values, weights, visible, alibi_bias)
        layer_out, puller = jax.vjp(forward, inputs, params)
        grad_inputs, grad_params = puller(cot_rows)
        updated = tuple((total_part + new_part for total_part, new_part in zip(gradient_sums, grad_params)))
        return (updated, (layer_out.astype(jnp.bfloat16), grad_inputs))
    starting = tuple((jnp.zeros_like(part) for part in params))
    gradient_sums, (outputs, grad_inputs) = lax.scan(advance, starting, (inputs_all, cotangents, lengths_all))
    return (outputs.reshape(-1, D), grad_inputs.reshape(-1, D), gradient_sums[0], gradient_sums[1], gradient_sums[2], gradient_sums[3], gradient_sums[4], gradient_sums[5], gradient_sums[6], gradient_sums[7], gradient_sums[8], gradient_sums[9], gradient_sums[10], gradient_sums[11])
```

```python
import functools
import math

import jax
import jax.numpy as jnp
from jax import lax
from jax.experimental import pallas as pl
from jax.experimental.pallas import tpu as pltpu
from jax.sharding import PartitionSpec as P

HEADS = 16
AXES = ("dp", "fsdp")
TILE = 128

epsilon = 1e-05
far_away = -1e33


def normalize(values, scaling, offset_vec):
    row_mean = jnp.mean(values, axis=-1, keepdims=True)
    centred = values - row_mean
    variance = jnp.mean(centred * centred, axis=-1, keepdims=True)
    return centred * lax.rsqrt(variance + epsilon) * scaling + offset_vec


def gelu_tanh(values):
    return jax.nn.gelu(values, approximate=True)


def across(left_side, right_side):
    return lax.dot_general(
        left_side, right_side, (((0,), (0,)), ((), ())), preferred_element_type=jnp.float32
    )


def against(left_side, right_side):
    return lax.dot_general(
        left_side, right_side, (((1,), (1,)), ((), ())), preferred_element_type=jnp.float32
    )


def device_bits():
    fsdp_bits = (lax.axis_size("fsdp") - 1).bit_length()
    total_bits = (lax.axis_size("dp") * lax.axis_size("fsdp") - 1).bit_length()
    inner = list(range(fsdp_bits))
    core = fsdp_bits
    outer = list(range(fsdp_bits + 1, total_bits))
    return inner, core, outer, total_bits


def swap(piece, bit, count):
    return lax.ppermute(piece, AXES, [(i, i ^ (1 << bit)) for i in range(count)])


def gather(shard, order):
    count = lax.axis_size("dp") * lax.axis_size("fsdp")
    bits = (count - 1).bit_length()
    index = lax.axis_index(AXES)
    held = shard.reshape((1,) * bits + shard.shape)
    for bit in order:
        axis = bits - 1 - bit
        got = swap(held, bit, count)
        upper = ((index >> bit) & 1) == 1
        held = jnp.concatenate(
            [jnp.where(upper, got, held), jnp.where(upper, held, got)], axis=axis
        )
    return held.reshape((count * shard.shape[0],) + shard.shape[1:])


def scatter_sum(whole, order, link_type):
    count = lax.axis_size("dp") * lax.axis_size("fsdp")
    bits = (count - 1).bit_length()
    index = lax.axis_index(AXES)
    held = whole.reshape((2,) * bits + (whole.shape[0] // count,) + whole.shape[1:])
    for step, bit in enumerate(order):
        axis = bits - 1 - bit
        mine = (index >> bit) & 1
        kept = lax.dynamic_slice_in_dim(held, mine, 1, axis)
        given = lax.dynamic_slice_in_dim(held, 1 - mine, 1, axis)
        got = swap(given.astype(link_type), bit, count)
        held = kept.astype(jnp.float32) + got.astype(jnp.float32)
        if step + 1 < len(order):
            held = held.astype(link_type)
    return held.reshape((whole.shape[0] // count,) + whole.shape[1:])


def distances(lengths_ref, buffer, rows):
    first = lengths_ref[buffer, 0]
    second = first + lengths_ref[buffer, 1]
    row = lax.broadcasted_iota(jnp.int32, (rows, rows), 0)
    col = lax.broadcasted_iota(jnp.int32, (rows, rows), 1)
    row_part = (row >= first).astype(jnp.int32) + (row >= second).astype(jnp.int32)
    col_part = (col >= first).astype(jnp.int32) + (col >= second).astype(jnp.int32)
    seen = (row_part == col_part) & (col <= row)
    return jnp.where(seen, (col - row).astype(jnp.float32), far_away)


def attend_kernel(lengths_ref, slopes_ref, q_ref, k_ref, v_ref, out_ref, probs_ref, far_ref):
    rows, width = q_ref.shape
    buffer, pair = pl.program_id(0), pl.program_id(1)

    @pl.when(pair == 0)
    def _():
        far_ref[...] = distances(lengths_ref, buffer, rows)

    lane = lax.broadcasted_iota(jnp.int32, (TILE, width), 1)
    low_half = lane < width // 2
    scale = 1.0 / math.sqrt(width // 2)
    for start in range(0, rows, TILE):
        stop = start + TILE
        q = q_ref[start:stop, :] * scale
        q = q.astype(jnp.bfloat16)
        results = []
        for head in range(2):
            picked = jnp.where(low_half == (head == 0), q, jnp.zeros_like(q))
            scores = against(picked, k_ref[:stop, :])
            scores = scores + slopes_ref[2 * pair + head] * far_ref[start:stop, :stop]
            peak = jnp.max(scores, axis=-1, keepdims=True)
            exponent = jnp.exp(scores - peak)
            total = jnp.sum(exponent, axis=-1, keepdims=True)
            probs = (exponent * (1.0 / total)).astype(jnp.bfloat16)
            probs_ref[0, head, start:stop, :stop] = probs
            results.append(
                jnp.dot(probs, v_ref[:stop, :], preferred_element_type=jnp.float32)
            )
        out_ref[start:stop, :] = jnp.where(low_half, results[0], results[1]).astype(jnp.bfloat16)


def attend(projected, lengths, slopes):
    rows, buffers = projected.shape[0], lengths.shape[0]
    block, width = rows // buffers, projected.shape[1] // 3
    pairs = HEADS // 2
    pair_width = width // pairs
    spec = lambda part: pl.BlockSpec((block, pair_width), lambda b, p: (b, part * pairs + p))
    smem = pl.BlockSpec(memory_space=pltpu.SMEM)
    return pl.pallas_call(
        attend_kernel,
        grid=(buffers, pairs),
        in_specs=[smem, smem, spec(0), spec(1), spec(2)],
        out_specs=[
            spec(0),
            pl.BlockSpec((1, 2, block, block), lambda b, p: (b, p, 0, 0)),
        ],
        out_shape=[
            jax.ShapeDtypeStruct((rows, width), jnp.bfloat16),
            jax.ShapeDtypeStruct((buffers, HEADS, block, block), jnp.bfloat16),
        ],
        scratch_shapes=[pltpu.VMEM((block, block), jnp.float32)],
        compiler_params=pltpu.CompilerParams(vmem_limit_bytes=32 * 2**20),
        cost_estimate=pl.CostEstimate(
            flops=4 * rows * block * width, bytes_accessed=16 * 2**20, transcendentals=0
        ),
    )(lengths, slopes, projected, projected, projected)


def attend_back_kernel(
    g_ref, probs_ref, q_ref, k_ref, v_ref, gq_ref, gk_ref, gv_ref, sums_ref, gk_sum, gv_sum
):
    rows, width = q_ref.shape
    scale = 1.0 / math.sqrt(width // 2)
    low_half = lax.broadcasted_iota(jnp.int32, (TILE, width), 1) < width // 2
    q_total = jnp.zeros((1, width), jnp.float32)
    gk_sum[...] = jnp.zeros_like(gk_sum)
    gv_sum[...] = jnp.zeros_like(gv_sum)
    for start in range(0, rows, TILE):
        stop = start + TILE
        g = g_ref[start:stop, :]
        q = (q_ref[start:stop, :] * scale).astype(jnp.bfloat16)
        gq = []
        for head in range(2):
            here = low_half == (head == 0)
            g_here = jnp.where(here, g, jnp.zeros_like(g))
            q_here = jnp.where(here, q, jnp.zeros_like(q))
            probs_low = probs_ref[0, head, start:stop, :stop]
            probs = probs_low.astype(jnp.float32)
            grad_probs = against(g_here, v_ref[:stop, :])
            inner = jnp.sum(probs * grad_probs, axis=-1, keepdims=True)
            grad_scores = (probs * (grad_probs - inner)).astype(jnp.bfloat16)
            gq.append(jnp.dot(grad_scores, k_ref[:stop, :], preferred_element_type=jnp.float32))
            gk_sum[:stop, :] += across(grad_scores, q_here)
            gv_sum[:stop, :] += across(probs_low, g_here)
        gq_block = jnp.where(low_half, gq[0], gq[1]) * scale
        q_total += jnp.sum(gq_block, axis=0, keepdims=True)
        gq_ref[start:stop, :] = gq_block.astype(jnp.bfloat16)
    gk_ref[...] = gk_sum[...].astype(jnp.bfloat16)
    gv_ref[...] = gv_sum[...].astype(jnp.bfloat16)
    sums_ref[0, 0:1, :] = q_total
    sums_ref[0, 1:2, :] = jnp.sum(gv_sum[...], axis=0, keepdims=True)


def attend_back(grad_attended, probs, projected):
    rows, buffers = projected.shape[0], probs.shape[0]
    block, width = rows // buffers, projected.shape[1] // 3
    pairs = HEADS // 2
    pair_width = width // pairs
    spec = lambda part: pl.BlockSpec((block, pair_width), lambda b, p: (b, part * pairs + p))
    flat = jax.ShapeDtypeStruct((rows, width), jnp.bfloat16)
    return pl.pallas_call(
        attend_back_kernel,
        grid=(buffers, pairs),
        in_specs=[
            spec(0),
            pl.BlockSpec((1, 2, block, block), lambda b, p: (b, p, 0, 0)),
            spec(0),
            spec(1),
            spec(2),
        ],
        out_specs=[
            spec(0),
            spec(0),
            spec(0),
            pl.BlockSpec((1, 2, pair_width), lambda b, p: (b, 0, p)),
        ],
        out_shape=[flat, flat, flat, jax.ShapeDtypeStruct((buffers, 2, width), jnp.float32)],
        scratch_shapes=[pltpu.VMEM((block, pair_width), jnp.float32)] * 2,
        compiler_params=pltpu.CompilerParams(vmem_limit_bytes=32 * 2**20),
        cost_estimate=pl.CostEstimate(
            flops=10 * rows * block * width, bytes_accessed=20 * 2**20, transcendentals=0
        ),
    )(grad_attended, probs, projected, projected, projected)


def local(
    tokens,
    lengths,
    cotangent,
    qkv_weight,
    query_value_bias,
    dense_weight,
    dense_bias,
    up_weight,
    up_bias,
    down_weight,
    down_bias,
    norm1_gain,
    norm1_shift,
    norm2_gain,
    norm2_shift,
):
    width = tokens.shape[1]
    inner, core, outer, bits = device_bits()
    outer_down = outer[::-1]
    gather_a = outer_down + inner[::-1] + [core]
    gather_b = outer_down[:-1] + inner[::-1] + outer_down[-1:] + [core]
    scatter_a, scatter_b = gather_a[::-1], gather_b[::-1]
    count = 1 << bits

    small = (
        query_value_bias,
        dense_bias,
        up_bias,
        down_bias,
        norm1_gain,
        norm1_shift,
        norm2_gain,
        norm2_shift,
    )
    sizes = [part.shape[0] for part in small]
    offsets = [sum(sizes[:i]) for i in range(len(sizes))]
    packed = gather(jnp.concatenate(small).reshape(1, -1), gather_b).astype(jnp.float32)
    b_qv, b_dense, b_up, b_down, gain_one, shift_one, gain_two, shift_two = [
        packed[:, at : at + size].reshape(-1) for at, size in zip(offsets, sizes)
    ]
    w_qkv = gather(qkv_weight, gather_a)
    w_dense = gather(dense_weight, gather_b)
    w_up = gather(up_weight, gather_a)
    w_down = gather(down_weight, gather_b)

    slopes = jnp.exp2(-8.0 * jnp.arange(1, HEADS + 1, dtype=jnp.float32) / HEADS)
    inputs = tokens.astype(jnp.float32)
    bias_full = jnp.concatenate([b_qv[:width], jnp.zeros((width,), jnp.float32), b_qv[width:]])
    normed_one = normalize(inputs, gain_one, shift_one).astype(jnp.bfloat16)
    projected = (
        jnp.dot(normed_one, w_qkv, preferred_element_type=jnp.float32) + bias_full
    ).astype(jnp.bfloat16)
    attended, probs = attend(projected, lengths, slopes)
    residual_mid = inputs + (
        jnp.dot(attended, w_dense, preferred_element_type=jnp.float32) + b_dense
    )
    normed_two = normalize(residual_mid, gain_two, shift_two).astype(jnp.bfloat16)
    upper_pre = jnp.dot(normed_two, w_up, preferred_element_type=jnp.float32) + b_up
    activated = gelu_tanh(upper_pre).astype(jnp.bfloat16)
    layer_out = residual_mid + (
        jnp.dot(activated, w_down, preferred_element_type=jnp.float32) + b_down
    )
    mixed = layer_out.astype(jnp.bfloat16)

    grad_float = cotangent.astype(jnp.float32)
    grad_down_weight = scatter_sum(
        across(activated, cotangent).astype(jnp.bfloat16), scatter_a, jnp.bfloat16
    )
    grad_down_bias = jnp.sum(grad_float, axis=0)
    grad_activated = against(cotangent, w_down)
    grad_upper = jax.vjp(gelu_tanh, upper_pre)[1](grad_activated)[0]
    grad_up_bias = jnp.sum(grad_upper, axis=0)
    grad_upper_low = grad_upper.astype(jnp.bfloat16)
    grad_up_weight = scatter_sum(
        across(normed_two, grad_upper_low).astype(jnp.bfloat16), scatter_b, jnp.bfloat16
    )
    grad_normed_two = against(grad_upper_low, w_up)
    grad_mid_part, grad_gain_two, grad_shift_two = jax.vjp(
        normalize, residual_mid, gain_two, shift_two
    )[1](grad_normed_two)
    grad_mid = grad_float + grad_mid_part
    grad_dense_bias = jnp.sum(grad_mid, axis=0)
    grad_mid_low = grad_mid.astype(jnp.bfloat16)
    grad_dense_weight = scatter_sum(
        across(attended, grad_mid_low).astype(jnp.bfloat16), scatter_a, jnp.bfloat16
    )
    grad_attended = against(grad_mid_low, w_dense).astype(jnp.bfloat16)
    grad_q, grad_k, grad_v, bias_sums = attend_back(grad_attended, probs, projected)
    grad_qv_bias = jnp.sum(bias_sums, axis=0).reshape(-1)
    grad_projected_low = jnp.concatenate([grad_q, grad_k, grad_v], axis=1)
    grad_qkv_weight = scatter_sum(
        across(normed_one, grad_projected_low).astype(jnp.bfloat16), scatter_b, jnp.bfloat16
    )
    grad_normed_one = against(grad_projected_low, w_qkv)
    grad_in_part, grad_gain_one, grad_shift_one = jax.vjp(
        normalize, inputs, gain_one, shift_one
    )[1](grad_normed_one)
    input_grad = grad_mid + grad_in_part

    small_grads = (
        grad_qv_bias,
        grad_dense_bias,
        grad_up_bias,
        grad_down_bias,
        grad_gain_one,
        grad_shift_one,
        grad_gain_two,
        grad_shift_two,
    )
    summed = scatter_sum(
        jnp.concatenate([part.reshape(count, -1) for part in small_grads], axis=1),
        scatter_a,
        jnp.float32,
    ).reshape(-1)
    (g_qv, g_dense, g_up, g_down, g_gain_one, g_shift_one, g_gain_two, g_shift_two) = [
        summed[at : at + size] for at, size in zip(offsets, sizes)
    ]
    return (
        mixed,
        input_grad,
        grad_qkv_weight,
        g_qv,
        grad_dense_weight,
        g_dense,
        grad_up_weight,
        g_up,
        grad_down_weight,
        g_down,
        g_gain_one,
        g_shift_one,
        g_gain_two,
        g_shift_two,
    )


def solution(mesh):
    rows, vector = P(AXES, None), P(AXES)
    return jax.shard_map(
        local,
        mesh=mesh,
        in_specs=(rows, rows, rows, rows, vector, rows, vector, rows, vector, rows)
        + (vector,) * 5,
        out_specs=(rows, rows, rows, vector, rows, vector, rows, vector, rows, vector)
        + (vector,) * 4,
        check_vma=False,
    )
```

```python
import functools
import math

import jax
import jax.numpy as jnp
from jax import lax
from jax.experimental import pallas as pl
from jax.experimental.pallas import tpu as pltpu
from jax.sharding import PartitionSpec as P

HEADS = 16
AXES = ("dp", "fsdp")
TILE = 128

epsilon = 1e-05
far_away = -1e33


def normalize(values, scaling, offset_vec):
    row_mean = jnp.mean(values, axis=-1, keepdims=True)
    centred = values - row_mean
    variance = jnp.mean(centred * centred, axis=-1, keepdims=True)
    return centred * lax.rsqrt(variance + epsilon) * scaling + offset_vec


def gelu_tanh(values):
    return jax.nn.gelu(values, approximate=True)


def across(left_side, right_side):
    return lax.dot_general(
        left_side, right_side, (((0,), (0,)), ((), ())), preferred_element_type=jnp.float32
    )


def against(left_side, right_side):
    return lax.dot_general(
        left_side, right_side, (((1,), (1,)), ((), ())), preferred_element_type=jnp.float32
    )


def device_bits():
    fsdp_bits = (lax.axis_size("fsdp") - 1).bit_length()
    total_bits = (lax.axis_size("dp") * lax.axis_size("fsdp") - 1).bit_length()
    inner = list(range(fsdp_bits))
    core = fsdp_bits
    outer = list(range(fsdp_bits + 1, total_bits))
    return inner, core, outer, total_bits


def swap(piece, bit, count):
    return lax.ppermute(piece, AXES, [(i, i ^ (1 << bit)) for i in range(count)])


def after(value, *others):
    return lax.optimization_barrier((value,) + others)[0]


def gather(shard, order, wait_for=None):
    count = lax.axis_size("dp") * lax.axis_size("fsdp")
    bits = (count - 1).bit_length()
    index = lax.axis_index(AXES)
    held = shard.reshape((1,) * bits + shard.shape)
    if wait_for is not None:
        held = after(held, wait_for)
    mark = held
    for step, bit in enumerate(order):
        axis = bits - 1 - bit
        got = swap(held, bit, count)
        side = jnp.arange(2).reshape((2,) + (1,) * (held.ndim - 1 - axis))
        held = jnp.where(side == (index >> bit) & 1, held, got)
        if step == len(order) - 4:
            mark = held
    return held.reshape((count * shard.shape[0],) + shard.shape[1:]), mark


class Sum:
    def __init__(self, whole, order, link_type):
        self.count = lax.axis_size("dp") * lax.axis_size("fsdp")
        self.bits = (self.count - 1).bit_length()
        self.index = lax.axis_index(AXES)
        self.shape = (whole.shape[0] // self.count,) + whole.shape[1:]
        self.held = whole.reshape((2,) * self.bits + self.shape)
        self.order, self.type = list(order), link_type

    def give(self):
        bit = self.order.pop(0)
        axis = self.bits - 1 - bit
        mine = (self.index >> bit) & 1
        self.kept = lax.dynamic_slice_in_dim(self.held, mine, 1, axis)
        given = lax.dynamic_slice_in_dim(self.held, 1 - mine, 1, axis)
        given = lax.optimization_barrier(given.astype(self.type))
        self.got = swap(given, bit, self.count)
        return given

    def take(self, *others):
        got = after(self.got, *others) if others else self.got
        self.held = self.kept.astype(jnp.float32) + got.astype(jnp.float32)
        if self.order:
            self.held = self.held.astype(self.type)

    def step(self, *others):
        self.take(*others)
        return self.give()

    def finish(self):
        while self.order:
            self.step()
        self.take()
        return self.held.reshape(self.shape)


def distances(lengths_ref, buffer, rows):
    first = lengths_ref[buffer, 0]
    second = first + lengths_ref[buffer, 1]
    row = lax.broadcasted_iota(jnp.int32, (rows, rows), 0)
    col = lax.broadcasted_iota(jnp.int32, (rows, rows), 1)
    row_part = (row >= first).astype(jnp.int32) + (row >= second).astype(jnp.int32)
    col_part = (col >= first).astype(jnp.int32) + (col >= second).astype(jnp.int32)
    seen = (row_part == col_part) & (col <= row)
    return jnp.where(seen, (col - row).astype(jnp.float32), far_away)


def attend_kernel(lengths_ref, slopes_ref, q_ref, k_ref, v_ref, out_ref, probs_ref, far_ref, *, first_head):
    rows, width = q_ref.shape
    buffer, pair = pl.program_id(0), pl.program_id(1)

    @pl.when(pair == 0)
    def _():
        far_ref[...] = distances(lengths_ref, buffer, rows)

    lane = lax.broadcasted_iota(jnp.int32, (TILE, width), 1)
    low_half = lane < width // 2
    scale = 1.0 / math.sqrt(width // 2)
    for start in range(0, rows, TILE):
        stop = start + TILE
        q = q_ref[start:stop, :] * scale
        q = q.astype(jnp.bfloat16)
        results = []
        for head in range(2):
            picked = jnp.where(low_half == (head == 0), q, jnp.zeros_like(q))
            scores = against(picked, k_ref[:stop, :])
            scores = scores + slopes_ref[first_head + 2 * pair + head] * far_ref[start:stop, :stop]
            peak = jnp.max(scores, axis=-1, keepdims=True)
            exponent = jnp.exp(scores - peak)
            total = jnp.sum(exponent, axis=-1, keepdims=True)
            probs = (exponent * (1.0 / total)).astype(jnp.bfloat16)
            probs_ref[0, head, start:stop, :stop] = probs
            results.append(
                jnp.dot(probs, v_ref[:stop, :], preferred_element_type=jnp.float32)
            )
        out_ref[start:stop, :] = jnp.where(low_half, results[0], results[1]).astype(jnp.bfloat16)


def attend(projected, lengths, slopes, first_head):
    rows, buffers = projected.shape[0], lengths.shape[0]
    block, width = rows // buffers, projected.shape[1] // 3
    pairs = HEADS // 4
    pair_width = width // pairs
    spec = lambda part: pl.BlockSpec((block, pair_width), lambda b, p: (b, part * pairs + p))
    smem = pl.BlockSpec(memory_space=pltpu.SMEM)
    return pl.pallas_call(
        functools.partial(attend_kernel, first_head=first_head),
        grid=(buffers, pairs),
        in_specs=[smem, smem, spec(0), spec(1), spec(2)],
        out_specs=[
            spec(0),
            pl.BlockSpec((1, 2, block, block), lambda b, p: (b, p, 0, 0)),
        ],
        out_shape=[
            jax.ShapeDtypeStruct((rows, width), jnp.bfloat16),
            jax.ShapeDtypeStruct((buffers, HEADS // 2, block, block), jnp.bfloat16),
        ],
        scratch_shapes=[pltpu.VMEM((block, block), jnp.float32)],
        compiler_params=pltpu.CompilerParams(vmem_limit_bytes=32 * 2**20),
        cost_estimate=pl.CostEstimate(
            flops=4 * rows * block * width, bytes_accessed=16 * 2**20, transcendentals=0
        ),
    )(lengths, slopes, projected, projected, projected)


def attend_back_kernel(
    g_ref, probs_ref, q_ref, k_ref, v_ref, gq_ref, gk_ref, gv_ref, sums_ref, gk_sum, gv_sum
):
    rows, width = q_ref.shape
    scale = 1.0 / math.sqrt(width // 2)
    low_half = lax.broadcasted_iota(jnp.int32, (TILE, width), 1) < width // 2
    q_total = jnp.zeros((1, width), jnp.float32)
    gk_sum[...] = jnp.zeros_like(gk_sum)
    gv_sum[...] = jnp.zeros_like(gv_sum)
    for start in range(0, rows, TILE):
        stop = start + TILE
        g = g_ref[start:stop, :]
        q = (q_ref[start:stop, :] * scale).astype(jnp.bfloat16)
        gq = []
        for head in range(2):
            here = low_half == (head == 0)
            g_here = jnp.where(here, g, jnp.zeros_like(g))
            q_here = jnp.where(here, q, jnp.zeros_like(q))
            probs_low = probs_ref[0, head, start:stop, :stop]
            probs = probs_low.astype(jnp.float32)
            grad_probs = against(g_here, v_ref[:stop, :])
            inner = jnp.sum(probs * grad_probs, axis=-1, keepdims=True)
            grad_scores = (probs * (grad_probs - inner)).astype(jnp.bfloat16)
            gq.append(jnp.dot(grad_scores, k_ref[:stop, :], preferred_element_type=jnp.float32))
            gk_sum[:stop, :] += across(grad_scores, q_here)
            gv_sum[:stop, :] += across(probs_low, g_here)
        gq_block = jnp.where(low_half, gq[0], gq[1]) * scale
        q_total += jnp.sum(gq_block, axis=0, keepdims=True)
        gq_ref[start:stop, :] = gq_block.astype(jnp.bfloat16)
    gk_ref[...] = gk_sum[...].astype(jnp.bfloat16)
    gv_ref[...] = gv_sum[...].astype(jnp.bfloat16)
    sums_ref[0, 0:1, :] = q_total
    sums_ref[0, 1:2, :] = jnp.sum(gv_sum[...], axis=0, keepdims=True)


def attend_back(grad_attended, probs, projected):
    rows, buffers = projected.shape[0], probs.shape[0]
    block, width = rows // buffers, projected.shape[1] // 3
    pairs = HEADS // 4
    pair_width = width // pairs
    spec = lambda part: pl.BlockSpec((block, pair_width), lambda b, p: (b, part * pairs + p))
    flat = jax.ShapeDtypeStruct((rows, width), jnp.bfloat16)
    return pl.pallas_call(
        attend_back_kernel,
        grid=(buffers, pairs),
        in_specs=[
            spec(0),
            pl.BlockSpec((1, 2, block, block), lambda b, p: (b, p, 0, 0)),
            spec(0),
            spec(1),
            spec(2),
        ],
        out_specs=[
            spec(0),
            spec(0),
            spec(0),
            pl.BlockSpec((1, 2, pair_width), lambda b, p: (b, 0, p)),
        ],
        out_shape=[flat, flat, flat, jax.ShapeDtypeStruct((buffers, 2, width), jnp.float32)],
        scratch_shapes=[pltpu.VMEM((block, pair_width), jnp.float32)] * 2,
        compiler_params=pltpu.CompilerParams(vmem_limit_bytes=32 * 2**20),
        cost_estimate=pl.CostEstimate(
            flops=10 * rows * block * width, bytes_accessed=20 * 2**20, transcendentals=0
        ),
    )(grad_attended, probs, projected, projected, projected)


def local(
    tokens,
    lengths,
    cotangent,
    qkv_weight,
    query_value_bias,
    dense_weight,
    dense_bias,
    up_weight,
    up_bias,
    down_weight,
    down_bias,
    norm1_gain,
    norm1_shift,
    norm2_gain,
    norm2_shift,
):
    width = tokens.shape[1]
    half = width // 2
    inner, core, outer, bits = device_bits()
    outer_down = outer[::-1]
    gather_a = outer_down + inner[::-1] + [core]
    gather_b = outer_down[:-1] + inner[::-1] + outer_down[-1:] + [core]
    scatter_a, scatter_b = gather_a[::-1], gather_b[::-1]
    count = 1 << bits

    small = (
        query_value_bias,
        dense_bias,
        up_bias,
        down_bias,
        norm1_gain,
        norm1_shift,
        norm2_gain,
        norm2_shift,
    )
    sizes = [part.shape[0] for part in small]
    offsets = [sum(sizes[:i]) for i in range(len(sizes))]

    def halves(array):
        parts = [array[..., i * half : (i + 1) * half] for i in range(array.shape[-1] // half)]
        return jnp.concatenate(parts[::2], axis=-1), jnp.concatenate(parts[1::2], axis=-1)

    qkv_first, qkv_second = halves(qkv_weight)
    packed, _ = gather(jnp.concatenate(small).reshape(1, -1), gather_b)
    packed = packed.astype(jnp.float32)
    b_qv, b_dense, b_up, b_down, gain_one, shift_one, gain_two, shift_two = [
        packed[:, at : at + size].reshape(-1) for at, size in zip(offsets, sizes)
    ]
    w_first, mark_first = gather(qkv_first, gather_a)
    w_second, mark_second = gather(
        jnp.concatenate([qkv_second, dense_weight], axis=1), gather_b
    )
    w_up, _ = gather(up_weight, gather_a, mark_first)
    w_down, _ = gather(down_weight, gather_b, mark_second)
    w_second, w_dense = w_second[:, : 3 * half], w_second[:, 3 * half :]

    slopes = jnp.exp2(-8.0 * jnp.arange(1, HEADS + 1, dtype=jnp.float32) / HEADS)
    inputs = tokens.astype(jnp.float32)
    bias_full = jnp.concatenate([b_qv[:width], jnp.zeros((width,), jnp.float32), b_qv[width:]])
    bias_halves = halves(bias_full)
    normed_one = normalize(inputs, gain_one, shift_one).astype(jnp.bfloat16)
    projected, attended, probs = [], [], []
    for part, weight in enumerate((w_first, w_second)):
        projected.append(
            (
                jnp.dot(normed_one, weight, preferred_element_type=jnp.float32)
                + bias_halves[part]
            ).astype(jnp.bfloat16)
        )
        out, kept = attend(projected[part], lengths, slopes, part * HEADS // 2)
        attended.append(out)
        probs.append(kept)
    attended = jnp.concatenate(attended, axis=1)
    residual_mid = inputs + (
        jnp.dot(attended, w_dense, preferred_element_type=jnp.float32) + b_dense
    )
    normed_two = normalize(residual_mid, gain_two, shift_two).astype(jnp.bfloat16)
    upper_pre = jnp.dot(normed_two, w_up, preferred_element_type=jnp.float32) + b_up
    activated = gelu_tanh(upper_pre).astype(jnp.bfloat16)

    grad_float = cotangent.astype(jnp.float32)
    down_sum = Sum(across(activated, cotangent).astype(jnp.bfloat16), scatter_a, jnp.bfloat16)
    sent = down_sum.give()
    grad_down_bias = jnp.sum(grad_float, axis=0)
    grad_activated = against(after(cotangent, sent), w_down)
    grad_upper = jax.vjp(gelu_tanh, upper_pre)[1](grad_activated)[0]
    grad_up_bias = jnp.sum(grad_upper, axis=0)
    grad_upper_low = grad_upper.astype(jnp.bfloat16)
    sent = down_sum.step(grad_upper_low)
    up_sum = Sum(
        across(after(normed_two, sent), grad_upper_low).astype(jnp.bfloat16),
        scatter_b,
        jnp.bfloat16,
    )
    sent = up_sum.give()
    grad_normed_two = against(after(grad_upper_low, sent), w_up)
    grad_mid_part, grad_gain_two, grad_shift_two = jax.vjp(
        normalize, residual_mid, gain_two, shift_two
    )[1](grad_normed_two)
    grad_mid = grad_float + grad_mid_part
    grad_dense_bias = jnp.sum(grad_mid, axis=0)
    grad_mid_low = grad_mid.astype(jnp.bfloat16)
    sent = up_sum.step(grad_mid_low)
    dense_grad = across(attended, after(grad_mid_low, sent)).astype(jnp.bfloat16)
    grad_attended = against(after(grad_mid_low, sent, dense_grad), w_dense).astype(jnp.bfloat16)
    first_back = attend_back(grad_attended[:, :half], probs[0], projected[0])
    first_low = jnp.concatenate(first_back[:3], axis=1)
    sent = down_sum.step(first_low)
    first_grad = across(after(normed_one, sent), first_low).astype(jnp.bfloat16)
    first_sum = Sum(
        jnp.concatenate([first_grad, dense_grad], axis=1), scatter_a, jnp.bfloat16
    )
    sent = first_sum.give()
    second_back = attend_back(after(grad_attended[:, half:], sent), probs[1], projected[1])
    second_low = jnp.concatenate(second_back[:3], axis=1)
    sent = (up_sum.step(second_low), down_sum.step(second_low))
    second_sum = Sum(
        across(after(normed_one, *sent), second_low).astype(jnp.bfloat16),
        scatter_b,
        jnp.bfloat16,
    )
    sent = (second_sum.give(),)
    bias_sums = [jnp.sum(back[3], axis=0) for back in (first_back, second_back)]
    grad_qv_bias = jnp.concatenate(
        [bias_sums[0][0], bias_sums[1][0], bias_sums[0][1], bias_sums[1][1]]
    )
    grad_normed_first = against(after(first_low, *sent), w_first)
    sent = (second_sum.step(grad_normed_first), first_sum.step(grad_normed_first))
    grad_normed_one = grad_normed_first + against(after(second_low, *sent), w_second)
    grad_in_part, grad_gain_one, grad_shift_one = jax.vjp(
        normalize, inputs, gain_one, shift_one
    )[1](grad_normed_one)
    input_grad = grad_mid + grad_in_part

    small_grads = (
        grad_qv_bias,
        grad_dense_bias,
        grad_up_bias,
        grad_down_bias,
        grad_gain_one,
        grad_shift_one,
        grad_gain_two,
        grad_shift_two,
    )
    small_sum = Sum(
        jnp.concatenate([part.reshape(count, -1) for part in small_grads], axis=1),
        scatter_a,
        jnp.float32,
    )
    sent = (
        small_sum.give(),
        second_sum.step(input_grad),
        up_sum.step(input_grad),
        down_sum.step(input_grad),
    )
    layer_out = residual_mid + (
        jnp.dot(after(activated, *sent), w_down, preferred_element_type=jnp.float32) + b_down
    )
    mixed = layer_out.astype(jnp.bfloat16)
    sent = (second_sum.step(mixed), first_sum.step(mixed), small_sum.step(mixed))

    grad_down_weight, grad_up_weight = down_sum.finish(), up_sum.finish()
    first_grad, second_grad = first_sum.finish(), second_sum.finish()
    summed = small_sum.finish().reshape(-1)
    grad_dense_weight = first_grad[:, 3 * half :]
    grad_qkv_weight = jnp.concatenate(
        [
            grad[:, i * half : (i + 1) * half]
            for i in range(3)
            for grad in (first_grad, second_grad)
        ],
        axis=1,
    )
    (g_qv, g_dense, g_up, g_down, g_gain_one, g_shift_one, g_gain_two, g_shift_two) = [
        summed[at : at + size] for at, size in zip(offsets, sizes)
    ]
    return (
        mixed,
        input_grad,
        grad_qkv_weight,
        g_qv,
        grad_dense_weight,
        g_dense,
        grad_up_weight,
        g_up,
        grad_down_weight,
        g_down,
        g_gain_one,
        g_shift_one,
        g_gain_two,
        g_shift_two,
    )


def solution(mesh):
    rows, vector = P(AXES, None), P(AXES)
    return jax.shard_map(
        local,
        mesh=mesh,
        in_specs=(rows, rows, rows, rows, vector, rows, vector, rows, vector, rows)
        + (vector,) * 5,
        out_specs=(rows, rows, rows, vector, rows, vector, rows, vector, rows, vector)
        + (vector,) * 4,
        check_vma=False,
    )
```
